32 devices in a mesh: row: 4 (over z), col: 8 (over y, x, core).
Axes of the slice: x: 2, y: 2, z: 4, core: 2. Of those that a mesh axis runs over, the one named last changes fastest.
Arguments:
- base_matrix: float32 [4096, 4096], P('row', 'col')
- inverse_factors: bfloat16 [128, 2, 512, 512], P(('row', 'col')), may hold values from -0.26516504 to 0.26516504
- coupling: bfloat16 [128, 2, 512, 256], P(('row', 'col')), may hold values from -0.36 to 0.36
- positions: int32 [128, 256], P(('row', 'col')), may hold values from 0 to 127, as said below
- counts: int32 [128, 4], P(('row', 'col')), may hold values from 1 to 64, as said below
- owners: int32 [128], P(('row', 'col')), may hold values from 0 to 7, as said below
Outputs:
- factored: float32 [4096, 4096], P('row', 'col')
The draws below stay inside these ranges and needn't reach their ends.
Inputs may be any that keep to these rules, and one draw needn't show every extreme that they name: Within each partition and each slot group of 64 slots, positions are distinct. `counts`: in every partition at least one slot group is fully used. `owners`: among the partitions held by the devices of one index of col, at most 4 share an owner, and exactly 4 do for some owner.
All inputs are finite; a program needn't handle non-finite values.
Results may differ from the reference program's by a relative error of at most 0.0003.
Values sent between devices are 32-bit elements; how exact they have to be, the bound alone decides.
A program may use at most 128 MiB of HBM per device.

```python
import jax
import jax.numpy as jnp
from jax import lax

TILE = 128
KS = 256
NB = 512
NBLK = 2
PART_DEV = 4
MOST = 4
PARTS_SIZE = 128
NG = 4096
ROWS_DEV = 1024
COLS_DEV = 512
SLOT = 64
N_ROW = 4
N_COL = 8


def draw_base_matrix(key, part):
    first_key, second_key = jax.random.split(jax.random.fold_in(key, 11))
    factor_key = jax.random.fold_in(key, 12)
    rank_width = 2 * TILE
    raw = 0.1 * jax.random.normal(first_key, (NG, NG), jnp.float32)
    diagonal = jax.random.uniform(second_key, (NG,), jnp.float32, 80.0, 120.0)
    factors = jax.random.normal(factor_key, (NG, rank_width), jnp.float32)
    factors = factors * (50.0 / rank_width) ** 0.5
    coupled = jnp.dot(factors, factors.T, precision=lax.Precision.HIGHEST)
    coupled = 0.5 * (coupled + coupled.T)
    symmetric = (raw + raw.T) * 0.7071
    unknown = jnp.arange(NG, dtype=jnp.int32)
    symmetric = jnp.where(unknown[:, None] == unknown[None, :], diagonal[:, None], symmetric)
    symmetric = symmetric + coupled
    stored = jnp.arange(NG, dtype=jnp.int32)
    local = stored % ROWS_DEV
    source = (local // TILE * N_ROW + stored // ROWS_DEV) * TILE + local % TILE
    return symmetric[source]


def bounded_field(key, shape, scale):
    first_key = jax.random.fold_in(key, 0)
    values = jnp.clip(jax.random.normal(first_key, shape, jnp.float32), -6.0, 6.0)
    return values * scale


def draw_inverse_factors(key, part):
    key = jax.random.fold_in(key, 51)
    return bounded_field(key, (PARTS_SIZE, NBLK, NB, NB), NB ** (-0.5)).astype(jnp.bfloat16)


def draw_coupling(key, part):
    key = jax.random.fold_in(key, 61)
    return bounded_field(key, (PARTS_SIZE, NBLK, NB, KS), 0.06).astype(jnp.bfloat16)


def draw_positions(key, part):
    scores = jax.random.randint(jax.random.fold_in(key, 21), (PARTS_SIZE, N_ROW, TILE), 0, 1 << 20) * TILE
    scores = scores + jnp.arange(TILE, dtype=jnp.int32)[None, None, :]
    order = jnp.argsort(scores, axis=-1).astype(jnp.int32)
    return order[:, :, :SLOT].reshape(PARTS_SIZE, KS)


def draw_counts(key, part):
    first_key, second_key = jax.random.split(jax.random.fold_in(key, 31))
    lowest = max(1, SLOT // 4)
    values = jax.random.randint(first_key, (PARTS_SIZE, N_ROW), lowest, SLOT + 1)
    full_group = jax.random.randint(second_key, (PARTS_SIZE,), 0, N_ROW)
    groups = jnp.arange(N_ROW, dtype=jnp.int32)
    return jnp.where(groups[None, :] == full_group[:, None], SLOT, values).astype(jnp.int32)


def draw_owners(key, part):
    first_key, second_key = jax.random.split(jax.random.fold_in(key, 41))
    items = N_ROW * PART_DEV
    crowded = items // (2 * MOST)
    heavy = crowded * MOST
    owner_scores = jax.random.randint(first_key, (N_COL, N_COL), 0, 1 << 20) * N_COL
    owner_perm = jnp.argsort(owner_scores + jnp.arange(N_COL, dtype=jnp.int32)[None, :], axis=1).astype(jnp.int32)
    item_scores = jax.random.randint(second_key, (N_COL, items), 0, 1 << 20) * items
    item_rank = jnp.argsort(item_scores + jnp.arange(items, dtype=jnp.int32)[None, :], axis=1).astype(jnp.int32)
    choice_index = jnp.where(item_rank < heavy, item_rank // MOST, crowded + (item_rank - heavy) % (N_COL - crowded))
    owned = jnp.take_along_axis(owner_perm, choice_index, axis=1)
    return owned.reshape(N_COL, N_ROW, PART_DEV).transpose(1, 0, 2).reshape(PARTS_SIZE).astype(jnp.int32)


def setup_inputs(seed: int = 0) -> dict:
    streams_of = jax.random.split(jax.random.key(seed), 7)
    base_matrix = draw_base_matrix(jax.random.fold_in(streams_of[6], 71), 0)
    inverse_factors = draw_inverse_factors(jax.random.fold_in(streams_of[6], 71), 0)
    coupling = draw_coupling(jax.random.fold_in(streams_of[6], 71), 0)
    positions = draw_positions(jax.random.fold_in(streams_of[6], 71), 0)
    counts = draw_counts(jax.random.fold_in(streams_of[6], 71), 0)
    owners = draw_owners(jax.random.fold_in(streams_of[6], 71), 0)
    return {"base_matrix": base_matrix, "inverse_factors": inverse_factors, "coupling": coupling, "positions": positions, "counts": counts, "owners": owners}


def stored_row(unknown):
    tile_number = unknown // TILE
    return tile_number % N_ROW * ROWS_DEV + tile_number // N_ROW * TILE + unknown % TILE

def row_unknowns():
    stored = jnp.arange(NG, dtype=jnp.int32)
    device = stored // ROWS_DEV
    local = stored % ROWS_DEV
    return (local // TILE * N_ROW + device) * TILE + local % TILE

def partition_schur(operands):
    inverse, couple, limits = operands
    factor = jnp.einsum('bij,bjk->bik', inverse.astype(jnp.float32), couple.astype(jnp.float32), precision=lax.Precision.HIGHEST).astype(jnp.bfloat16)
    wide = factor.astype(jnp.float32)
    product = jnp.einsum('bik,bil->kl', wide, wide, precision=lax.Precision.HIGHEST)
    slot_group = jnp.arange(KS, dtype=jnp.int32) // SLOT
    usable = (jnp.arange(KS, dtype=jnp.int32) % SLOT < limits[slot_group]).astype(product.dtype)
    return product * usable[:, None] * usable[None, :]

def panel(matrix, panel_index, row_unknown):
    column_block = matrix[:, panel_index * TILE:(panel_index + 1) * TILE]
    top = panel_index * ROWS_DEV
    diagonal = column_block[top:top + TILE]
    lower = jnp.linalg.cholesky(diagonal)
    identity = jnp.eye(TILE, dtype=matrix.dtype)
    inverse = lax.linalg.triangular_solve(lower, identity, left_side=True, lower=True)
    solved = jnp.dot(column_block, inverse.T, precision=lax.Precision.HIGHEST)
    tile_values = lower[row_unknown % TILE]
    in_tile = row_unknown // TILE == panel_index
    below = row_unknown >= (panel_index + 1) * TILE
    rows_part = jnp.where(in_tile[:, None], tile_values, jnp.where(below[:, None], solved, jnp.zeros_like(solved)))
    cols_part = rows_part[stored_row(jnp.arange(NG, dtype=jnp.int32))]
    return (rows_part, cols_part)

def reference(base_matrix, inverse_factors, coupling, positions, counts, owners):
    schur_rows = lax.map(partition_schur, (inverse_factors, coupling, counts))
    slot_group = jnp.arange(KS, dtype=jnp.int32) // SLOT
    unknown = owners[:, None] * COLS_DEV + slot_group[None, :] * TILE + positions
    rows = stored_row(unknown)
    assembled = base_matrix.at[rows[:, :, None], unknown[:, None, :]].add(-schur_rows)
    row_unknown = row_unknowns()
    first_rows, first_cols = panel(assembled, 0, row_unknown)
    updated = assembled - jnp.dot(first_rows, first_cols.T, precision=lax.Precision.HIGHEST)
    second_rows, second_cols = panel(updated, 1, row_unknown)
    trailing = updated - jnp.dot(second_rows, second_cols.T, precision=lax.Precision.HIGHEST)
    factored = trailing.at[:, :TILE].set(first_rows).at[:, TILE:2 * TILE].set(second_rows)
    column = jnp.arange(NG, dtype=jnp.int32)
    blank = (row_unknown < 2 * TILE)[:, None] & (column >= 2 * TILE)[None, :]
    return jnp.where(blank, jnp.zeros_like(factored), factored)
```

```python
import functools

import jax
import jax.numpy as jnp
from jax import lax
from jax.experimental import pallas as pl
from jax.experimental.pallas import tpu as pltpu
from jax.sharding import PartitionSpec as P

TILE = 128
KS = 256
PANEL = 2 * TILE
VMEM_BYTES = 50 * 1024 * 1024
MESH = pl.DeviceIdType.MESH
NT = (((1,), (1,)), ((), ()))
NN = (((1,), (0,)), ((), ()))


def exchange_kernel(
    n_row,
    n_col,
    part_dev,
    base_ref,
    pieces_ref,
    labels_ref,
    raw_ref,
    q_ref,
    diag_ref,
    top_ref,
    tile_ref,
    got,
    got_labels,
    wide_hi,
    wide_lo,
    partial,
    landed,
    piece_send,
    piece_recv,
    label_send,
    label_recv,
    raw_send,
    raw_recv,
    q_send,
    q_recv,
    part_send,
    part_recv,
    diag_send,
    diag_recv,
    top_send,
    top_recv,
    local_sem,
):
    r = lax.axis_index("row")
    c = lax.axis_index("col")
    width = KS // n_row
    cols_dev = n_row * TILE

    def row_peer(d):
        return lax.rem(r + d, n_row)

    def row_source(d):
        return lax.rem(r + n_row - d, n_row)

    def col_peer(d):
        return lax.rem(c + d, n_col)

    def col_source(d):
        return lax.rem(c + n_col - d, n_col)

    barrier = pltpu.get_barrier_semaphore()
    for d in range(1, n_row):
        pl.semaphore_signal(barrier, inc=1, device_id={"row": row_peer(d)}, device_id_type=MESH)
    for d in range(1, n_col):
        pl.semaphore_signal(barrier, inc=1, device_id={"col": col_peer(d)}, device_id_type=MESH)
    pl.semaphore_wait(barrier, n_row + n_col - 2)

    def piece_copy(to, slot):
        return pltpu.make_async_remote_copy(
            src_ref=pieces_ref.at[to],
            dst_ref=got.at[slot],
            send_sem=piece_send.at[to],
            recv_sem=piece_recv.at[slot],
            device_id={"row": to},
            device_id_type=MESH,
        )

    def label_copy(to, slot):
        return pltpu.make_async_remote_copy(
            src_ref=labels_ref.at[to],
            dst_ref=got_labels.at[slot],
            send_sem=label_send.at[to],
            recv_sem=label_recv.at[slot],
            device_id={"row": to},
            device_id_type=MESH,
        )

    def raw_copy(to):
        return pltpu.make_async_remote_copy(
            src_ref=base_ref.at[:, pl.ds(0, PANEL)],
            dst_ref=raw_ref,
            send_sem=raw_send.at[to],
            recv_sem=raw_recv,
            device_id={"col": to},
            device_id_type=MESH,
        )

    def q_copy(to, half):
        return pltpu.make_async_remote_copy(
            src_ref=q_ref.at[pl.ds(half * TILE, TILE)],
            dst_ref=q_ref.at[pl.ds(half * TILE, TILE)],
            send_sem=q_send.at[to],
            recv_sem=q_recv.at[half],
            device_id={"row": to},
            device_id_type=MESH,
        )

    def part_copy(to, slot):
        return pltpu.make_async_remote_copy(
            src_ref=partial.at[to],
            dst_ref=landed.at[slot],
            send_sem=part_send.at[to],
            recv_sem=part_recv.at[slot],
            device_id={"col": to},
            device_id_type=MESH,
        )

    def diag_copy(to):
        return pltpu.make_async_remote_copy(
            src_ref=diag_ref,
            dst_ref=diag_ref,
            send_sem=diag_send.at[to],
            recv_sem=diag_recv,
            device_id={"col": to},
            device_id_type=MESH,
        )

    def top_copy(to):
        return pltpu.make_async_remote_copy(
            src_ref=top_ref,
            dst_ref=top_ref,
            send_sem=top_send.at[to],
            recv_sem=top_recv,
            device_id={"col": to},
            device_id_type=MESH,
        )

    for d in range(1, n_row):
        label_copy(row_peer(d), r).start()
    for d in range(1, n_row):
        piece_copy(row_peer(d), r).start()
    own_piece = pltpu.make_async_copy(pieces_ref.at[r], got.at[r], local_sem.at[0])
    own_label = pltpu.make_async_copy(labels_ref.at[r], got_labels.at[r], local_sem.at[1])
    own_piece.start()
    own_label.start()

    @pl.when(c == 0)
    def _():
        for to in range(1, n_col):
            raw_copy(to).start()
        own_raw = pltpu.make_async_copy(
            base_ref.at[:, pl.ds(0, PANEL)], raw_ref, local_sem.at[2]
        )
        own_raw.start()
        own_raw.wait()

    own_tile = pltpu.make_async_copy(
        base_ref.at[pl.ds(c * TILE, TILE)], tile_ref, local_sem.at[3]
    )
    own_tile.start()

    own_piece.wait()
    own_label.wait()

    def widen(src):
        for p in range(part_dev):
            block = got[src, pl.ds(p * width, width), :]
            high = block.astype(jnp.bfloat16)
            low = (block - high.astype(jnp.float32)).astype(jnp.bfloat16)
            code = got_labels[src, pl.ds(p, 1), :]
            spot = lax.broadcasted_iota(jnp.int32, (cols_dev, KS), 0)
            onehot = jnp.where(spot == code, 1.0, 0.0).astype(jnp.bfloat16)
            both = jnp.concatenate([high, low], axis=0)
            out = lax.dot_general(both, onehot, NT, preferred_element_type=jnp.float32)
            out = out.astype(jnp.bfloat16)
            wide_hi[src, pl.ds(p * width, width), :] = out[:width]
            wide_lo[src, pl.ds(p * width, width), :] = out[width:]

    widen(r)

    def arrive(d, carry):
        src = lax.rem(r + n_row - d, n_row)
        label_copy(row_peer(1), src).wait_recv()
        piece_copy(row_peer(1), src).wait_recv()
        widen(src)
        return carry

    lax.fori_loop(1, n_row, arrive, 0)

    def send_q(half):
        for d in range(1, n_row):
            q_copy(row_peer(d), half).start()

    for half in range(2):

        @pl.when((r == half) & (c != 0))
        def _():
            own_q = pltpu.make_async_copy(
                base_ref.at[pl.ds(0, TILE)], q_ref.at[pl.ds(half * TILE, TILE)], local_sem.at[4]
            )
            own_q.start()
            own_q.wait()
            send_q(half)

    def gather_owner(o, carry):
        total = jnp.zeros((TILE, cols_dev), jnp.float32)
        for src in range(n_row):
            code = got_labels[src, pl.ds(part_dev, 1), :][:, : part_dev * width]
            spot = lax.broadcasted_iota(jnp.int32, (TILE, part_dev * width), 0) + o * TILE
            onehot = jnp.where(spot == code, 1.0, 0.0).astype(jnp.bfloat16)
            total += lax.dot_general(onehot, wide_hi[src], NN, preferred_element_type=jnp.float32)
            total += lax.dot_general(onehot, wide_lo[src], NN, preferred_element_type=jnp.float32)
        partial[o] = total

        @pl.when(o != c)
        def _():
            part_copy(o, c).start()

        return carry

    lax.fori_loop(0, n_col, gather_owner, 0)

    own_tile.wait()
    summed = partial[c]
    for d in range(1, n_col):
        src = col_source(d)
        part_copy(col_peer(1), src).wait_recv()
        summed += landed[src]
    tile_ref[...] = tile_ref[...] - summed

    for half in range(2):

        @pl.when((r == half) & (c == 0))
        def _():
            q_ref[pl.ds(half * TILE, TILE), :] = tile_ref[...]
            send_q(half)

    @pl.when(c == 0)
    def _():
        top_ref[...] = tile_ref[:, :PANEL]

    for half in range(2):

        @pl.when(r != half)
        def _():
            q_copy(row_peer(1), half).wait_recv()

    @pl.when(c == 0)
    def _():
        diag_ref[...] = q_ref[:, :PANEL]
        for to in range(1, n_col):
            diag_copy(to).start()
        for to in range(1, n_col):
            top_copy(to).start()

    @pl.when(c != 0)
    def _():
        diag_copy(0).wait_recv()
        top_copy(0).wait_recv()
        raw_copy(0).wait_recv()

    @pl.when(c == 0)
    def _():
        for to in range(1, n_col):
            diag_copy(to).wait_send()
            top_copy(to).wait_send()
            raw_copy(to).wait_send()

    for d in range(1, n_row):
        label_copy(row_peer(d), r).wait_send()
        piece_copy(row_peer(d), r).wait_send()
    for d in range(1, n_col):
        part_copy(col_peer(d), c).wait_send()
    for half in range(2):

        @pl.when(r == half)
        def _():
            for d in range(1, n_row):
                q_copy(row_peer(d), half).wait_send()


def exchange(n_row, n_col, base, pieces, labels):
    rows_dev, cols_dev = base.shape
    part_dev = pieces.shape[1] // (KS // n_row)
    any_spec = pl.BlockSpec(memory_space=pl.ANY)
    vmem_spec = pl.BlockSpec(memory_space=pltpu.VMEM)
    dma = pltpu.SemaphoreType.DMA
    return pl.pallas_call(
        functools.partial(exchange_kernel, n_row, n_col, part_dev),
        out_shape=(
            jax.ShapeDtypeStruct((rows_dev, PANEL), jnp.float32),
            jax.ShapeDtypeStruct((PANEL, cols_dev), jnp.float32),
            jax.ShapeDtypeStruct((PANEL, PANEL), jnp.float32),
            jax.ShapeDtypeStruct((TILE, PANEL), jnp.float32),
            jax.ShapeDtypeStruct((TILE, cols_dev), jnp.float32),
        ),
        in_specs=[any_spec, vmem_spec, vmem_spec],
        out_specs=(any_spec, vmem_spec, vmem_spec, vmem_spec, vmem_spec),
        scratch_shapes=[
            pltpu.VMEM((n_row, KS * part_dev // n_row, KS), jnp.float32),
            pltpu.VMEM(labels.shape, jnp.int32),
            pltpu.VMEM((n_row, KS * part_dev // n_row, cols_dev), jnp.bfloat16),
            pltpu.VMEM((n_row, KS * part_dev // n_row, cols_dev), jnp.bfloat16),
            pltpu.VMEM((n_col, TILE, cols_dev), jnp.float32),
            pltpu.VMEM((n_col, TILE, cols_dev), jnp.float32),
            dma((n_row,)),
            dma((n_row,)),
            dma((n_row,)),
            dma((n_row,)),
            dma((n_col,)),
            dma,
            dma((n_row,)),
            dma((2,)),
            dma((n_col,)),
            dma((n_col,)),
            dma((n_col,)),
            dma,
            dma((n_col,)),
            dma,
            dma((5,)),
        ],
        compiler_params=pltpu.CompilerParams(
            collective_id=0, has_side_effects=True, vmem_limit_bytes=VMEM_BYTES
        ),
    )(base, pieces, labels)


def full_dot(a, b, dims):
    return lax.dot_general(
        a, b, dims, precision=lax.Precision.HIGHEST, preferred_element_type=jnp.float32
    )


def split_dot(a, b, dims):
    a_high = a.astype(jnp.bfloat16)
    a_low = (a - a_high.astype(jnp.float32)).astype(jnp.bfloat16)
    b_high = b.astype(jnp.bfloat16)
    b_low = (b - b_high.astype(jnp.float32)).astype(jnp.bfloat16)
    dot = functools.partial(
        lax.dot_general, dimension_numbers=dims, preferred_element_type=jnp.float32
    )
    return dot(a_high, b_high) + (dot(a_high, b_low) + dot(a_low, b_high))


STEP = 4


def cholesky_and_inverse(work, block):
    row = lax.broadcasted_iota(jnp.int32, (TILE, TILE), 0)
    col = lax.broadcasted_iota(jnp.int32, (TILE, TILE), 1)
    groups = TILE // 8
    left = block.reshape(groups, 8, TILE)
    right = jnp.where(row == col, 1.0, 0.0).reshape(groups, 8, TILE)
    for k in range(0, TILE, STEP):
        g = k // 8
        s = k % 8
        lanes_left = [
            jnp.broadcast_to(left[0:1, s + i : s + i + 1, :], (1, 8, TILE)) for i in range(STEP)
        ]
        lanes_right = [
            jnp.broadcast_to(right[0:1, s + i : s + i + 1, :], (1, 8, TILE)) for i in range(STEP)
        ]
        cols = [
            jnp.broadcast_to(left[:, :, k + i : k + i + 1], left.shape) for i in range(STEP)
        ]
        heads = [
            [
                jnp.broadcast_to(cols[j][0:1, s + i : s + i + 1, :], (1, 8, TILE))
                for j in range(i + 1)
            ]
            for i in range(STEP)
        ]
        for i in range(STEP):
            scale = lax.rsqrt(heads[i][i])
            lanes_left[i] = lanes_left[i] * scale
            lanes_right[i] = lanes_right[i] * scale
            cols[i] = cols[i] * scale
            below = {}
            for m in range(i + 1, STEP):
                below[m] = heads[m][i] * scale
            for m in range(i + 1, STEP):
                for j in range(i + 1, m + 1):
                    heads[m][j] = heads[m][j] - below[m] * below[j]
                lanes_left[m] = lanes_left[m] - below[m] * lanes_left[i]
                lanes_right[m] = lanes_right[m] - below[m] * lanes_right[i]
                cols[m] = cols[m] - cols[i] * below[m]
        for i in range(STEP):
            work[k + i : k + i + 1, :TILE] = lanes_left[i][0, 0:1, :]
            work[k + i : k + i + 1, TILE:] = lanes_right[i][0, 0:1, :]
        if s + STEP == 8:
            left, right = left[1:], right[1:]
            cols = [x[1:] for x in cols]
        if left.shape[0]:
            for i in range(STEP):
                left = left - cols[i] * lanes_left[i]
                right = right - cols[i] * lanes_right[i]
    upper = jnp.where(row <= col, work[:, :TILE], 0.0)
    inverse = jnp.where(row >= col, work[:, TILE:], 0.0)
    return upper.T, inverse


def factor_kernel(
    base_ref, raw_ref, q_ref, diag_ref, top_ref, tile_ref, out_ref, work, inverse, panel, q_full
):
    r = lax.axis_index("row")
    c = lax.axis_index("col")
    rows_dev, cols_dev = base_ref.shape
    lower0, inverse0 = cholesky_and_inverse(work, diag_ref[:TILE, :TILE])
    lower10 = full_dot(diag_ref[TILE:, :TILE], inverse0, NT)
    lower1, inverse1 = cholesky_and_inverse(
        work, diag_ref[TILE:, TILE:] - full_dot(lower10, lower10, NT)
    )
    inverse[:TILE, :TILE] = inverse0
    inverse[:TILE, TILE:] = jnp.zeros((TILE, TILE), jnp.float32)
    inverse[TILE:, TILE:] = inverse1
    inverse[TILE:, :TILE] = -full_dot(inverse1, full_dot(lower10, inverse0, NN), NN)
    q_full[...] = full_dot(inverse[...], q_ref[...], NN)
    raw_ref[:TILE, :] = top_ref[...]

    def rows(i, carry):
        at = pl.ds(pl.multiple_of(i * TILE, TILE), TILE)
        panel[at, :] = split_dot(raw_ref[at, :], inverse[...], NT)
        return carry

    lax.fori_loop(0, rows_dev // TILE, rows, 0)

    @pl.when(r == 0)
    def _():
        panel[:TILE, :TILE] = lower0
        panel[:TILE, TILE:] = jnp.zeros((TILE, TILE), jnp.float32)

    @pl.when(r == 1)
    def _():
        panel[:TILE, :TILE] = lower10
        panel[:TILE, TILE:] = lower1

    def trailing(i, carry):
        at = pl.ds(pl.multiple_of(i * TILE, TILE), TILE)
        current = jnp.where(i == c, tile_ref[...], base_ref[at, :])
        out_ref[at, :] = current - split_dot(panel[at, :], q_full[...], NN)
        return carry

    lax.fori_loop(0, rows_dev // TILE, trailing, 0)

    @pl.when(r < 2)
    def _():
        out_ref[:TILE, :] = jnp.zeros((TILE, cols_dev), jnp.float32)

    @pl.when(c == 0)
    def _():
        out_ref[:, :PANEL] = panel[...]


def factorise(base, raw, q, diag, top, tile):
    rows_dev, cols_dev = base.shape
    vmem_spec = pl.BlockSpec(memory_space=pltpu.VMEM)
    return pl.pallas_call(
        factor_kernel,
        out_shape=jax.ShapeDtypeStruct(base.shape, jnp.float32),
        in_specs=[vmem_spec] * 6,
        out_specs=vmem_spec,
        scratch_shapes=[
            pltpu.VMEM((TILE, 2 * TILE), jnp.float32),
            pltpu.VMEM((PANEL, PANEL), jnp.float32),
            pltpu.VMEM((rows_dev, PANEL), jnp.float32),
            pltpu.VMEM((PANEL, cols_dev), jnp.float32),
        ],
        compiler_params=pltpu.CompilerParams(vmem_limit_bytes=VMEM_BYTES),
    )(base, raw, q, diag, top, tile)


def local(base_matrix, inverse_factors, coupling, positions, counts, owners):
    n_row = lax.axis_size("row")
    n_col = lax.axis_size("col")
    part_dev = coupling.shape[0]
    width = KS // n_row
    factor = jnp.einsum(
        "pbij,pbjk->pbik", inverse_factors, coupling, preferred_element_type=jnp.float32
    ).astype(jnp.bfloat16)
    schur_rows = jnp.einsum("pbik,pbil->pkl", factor, factor, preferred_element_type=jnp.float32)
    pieces = schur_rows.reshape(part_dev, n_row, width, KS).transpose(1, 0, 2, 3)
    pieces = pieces.reshape(n_row, part_dev * width, KS)
    within = jnp.arange(width, dtype=jnp.int32)
    group = jnp.arange(n_row, dtype=jnp.int32)
    usable = within[None, None, :] < counts[:, :, None]
    place = positions.reshape(part_dev, n_row, width)
    col_code = jnp.where(usable, group[None, :, None] * TILE + place, -1).reshape(part_dev, KS)
    row_code = jnp.where(usable, owners[:, None, None] * TILE + place, -1)
    row_code = row_code.transpose(1, 0, 2).reshape(n_row, 1, part_dev * width)
    labels = jnp.concatenate(
        [
            jnp.broadcast_to(col_code[None], (n_row, part_dev, KS)),
            jnp.pad(row_code, ((0, 0), (0, 0), (0, KS - part_dev * width))),
            jnp.zeros((n_row, 7 - part_dev, KS), jnp.int32),
        ],
        axis=1,
    )
    raw, q, diag, top, tile = exchange(n_row, n_col, base_matrix, pieces, labels)
    return factorise(base_matrix, raw, q, diag, top, tile)


def solution(mesh):
    in_specs = (
        P("row", "col"),
        P(("row", "col"), None, None, None),
        P(("row", "col"), None, None, None),
        P(("row", "col"), None),
        P(("row", "col"), None),
        P(("row", "col")),
    )
    out_specs = P("row", "col")
    return jax.shard_map(local, mesh=mesh, in_specs=in_specs, out_specs=out_specs, check_vma=False)
```

```python
import functools

import jax
import jax.numpy as jnp
from jax import lax
from jax.experimental import pallas as pl
from jax.experimental.pallas import tpu as pltpu
from jax.sharding import PartitionSpec as P

TILE = 128
KS = 256
PANEL = 2 * TILE
VMEM_BYTES = 50 * 1024 * 1024
MESH = pl.DeviceIdType.MESH
NT = (((1,), (1,)), ((), ()))
NN = (((1,), (0,)), ((), ()))


def exchange_kernel(
    n_row,
    n_col,
    part_dev,
    base_ref,
    pieces_ref,
    labels_ref,
    raw_ref,
    q_ref,
    diag_ref,
    top_ref,
    tile_ref,
    got,
    got_labels,
    wide_hi,
    wide_lo,
    partial,
    paired,
    landed,
    piece_send,
    piece_recv,
    label_send,
    label_recv,
    raw_send,
    raw_recv,
    q_send,
    q_recv,
    pair_send,
    pair_recv,
    part_send,
    part_recv,
    deal_send,
    top_send,
    top_recv,
    lift_send,
    lift_recv,
    diag_send,
    diag_recv,
    local_sem,
):
    r = lax.axis_index("row")
    c = lax.axis_index("col")
    width = KS // n_row
    cols_dev = n_row * TILE
    chunk = TILE // n_col
    parity = lax.rem(c, 2)
    twin = c + 1 - 2 * parity
    pairs = n_col // 2
    place = lax.div(c, 2)

    def row_peer(d):
        return lax.rem(r + d, n_row)

    def col_peer(d):
        return lax.rem(c + d, n_col)

    def send(src, dst, send_sem, recv_sem, axis, to):
        return pltpu.make_async_remote_copy(
            src_ref=src,
            dst_ref=dst,
            send_sem=send_sem,
            recv_sem=recv_sem,
            device_id={axis: to},
            device_id_type=MESH,
        )

    def piece_copy(to, slot):
        return send(
            pieces_ref.at[to], got.at[slot], piece_send.at[to], piece_recv.at[slot], "row", to
        )

    def label_copy(to, slot):
        return send(
            labels_ref.at[to], got_labels.at[slot], label_send.at[to], label_recv.at[slot], "row", to
        )

    def raw_deal(to):
        at = pl.ds(to * TILE, TILE)
        return send(
            base_ref.at[at, pl.ds(0, PANEL)],
            raw_ref.at[at],
            raw_send.at[to],
            raw_recv.at[to],
            "col",
            to,
        )

    def raw_copy(to, index):
        at = pl.ds(index * TILE, TILE)
        return send(
            raw_ref.at[at], raw_ref.at[at], raw_send.at[to], raw_recv.at[index], "col", to
        )

    def q_copy(to, half):
        at = pl.ds(half * TILE, TILE)
        return send(q_ref.at[at], q_ref.at[at], q_send.at[to], q_recv.at[half], "row", to)

    def q_rest_copy(to, half):
        at = q_ref.at[pl.ds(half * TILE, TILE), pl.ds(PANEL, cols_dev - PANEL)]
        return send(at, at, q_send.at[to], q_recv.at[half], "row", to)

    def pair_copy(j):
        owner = 2 * j + 1 - parity
        return send(partial.at[owner], paired.at[j], pair_send.at[j], pair_recv.at[j], "col", twin)

    def part_copy(j, slot):
        owner = 2 * j + parity
        return send(
            partial.at[owner], landed.at[slot], part_send.at[j], part_recv.at[slot], "col", owner
        )

    def deal_copy(to):
        at = top_ref.at[pl.ds(to * chunk, chunk)]
        return send(at, at, deal_send.at[to], top_recv.at[to], "col", to)

    def top_copy(to, index):
        at = top_ref.at[pl.ds(index * chunk, chunk)]
        return send(at, at, top_send.at[to], top_recv.at[index], "col", to)

    def lift_copy(to, half):
        return send(
            top_ref.at[pl.ds(c * chunk, chunk)],
            diag_ref.at[pl.ds(half * TILE + c * chunk, chunk)],
            lift_send.at[to],
            lift_recv.at[half],
            "row",
            to,
        )

    def diag_copy(to, half, index):
        at = diag_ref.at[pl.ds(half * TILE + index * chunk, chunk)]
        return send(at, at, diag_send.at[half, to], diag_recv.at[half, index], "col", to)

    barrier = pltpu.get_barrier_semaphore()
    for d in range(1, n_row):
        pl.semaphore_signal(barrier, inc=1, device_id={"row": row_peer(d)}, device_id_type=MESH)
    for d in range(1, n_col):
        pl.semaphore_signal(barrier, inc=1, device_id={"col": col_peer(d)}, device_id_type=MESH)
    pl.semaphore_wait(barrier, n_row + n_col - 2)

    for d in range(1, n_row):
        label_copy(row_peer(d), r).start()
    for d in range(1, n_row):
        piece_copy(row_peer(d), r).start()
    own_piece = pltpu.make_async_copy(pieces_ref.at[r], got.at[r], local_sem.at[0])
    own_label = pltpu.make_async_copy(labels_ref.at[r], got_labels.at[r], local_sem.at[1])
    own_piece.start()
    own_label.start()
    own_tile = pltpu.make_async_copy(
        base_ref.at[pl.ds(c * TILE, TILE)], tile_ref, local_sem.at[3]
    )
    own_tile.start()

    @pl.when(c == 0)
    def _():
        for to in range(1, n_col):
            raw_deal(to).start()
        own_raw = pltpu.make_async_copy(
            base_ref.at[:, pl.ds(0, PANEL)], raw_ref, local_sem.at[2]
        )
        own_raw.start()
        own_raw.wait()

    own_piece.wait()
    own_label.wait()

    def widen(src):
        for p in range(part_dev):
            block = got[src, pl.ds(p * width, width), :]
            high = block.astype(jnp.bfloat16)
            low = (block - high.astype(jnp.float32)).astype(jnp.bfloat16)
            code = got_labels[src, pl.ds(p, 1), :]
            spot = lax.broadcasted_iota(jnp.int32, (cols_dev, KS), 0)
            onehot = jnp.where(spot == code, 1.0, 0.0).astype(jnp.bfloat16)
            both = jnp.concatenate([high, low], axis=0)
            out = lax.dot_general(both, onehot, NT, preferred_element_type=jnp.float32)
            out = out.astype(jnp.bfloat16)
            wide_hi[src, pl.ds(p * width, width), :] = out[:width]
            wide_lo[src, pl.ds(p * width, width), :] = out[width:]

    widen(r)

    @pl.when(c != 0)
    def _():
        raw_copy(0, c).wait_recv()
        for d in range(1, n_col):
            to = col_peer(d)

            @pl.when(to != 0)
            def _():
                raw_copy(to, c).start()

    def arrive(d, carry):
        src = lax.rem(r + n_row - d, n_row)
        label_copy(row_peer(1), src).wait_recv()
        piece_copy(row_peer(1), src).wait_recv()
        widen(src)
        return carry

    lax.fori_loop(1, n_row, arrive, 0)

    for half in range(2):

        @pl.when((r == half) & (c != 0))
        def _():
            own_q = pltpu.make_async_copy(
                base_ref.at[pl.ds(0, TILE)], q_ref.at[pl.ds(half * TILE, TILE)], local_sem.at[4]
            )
            own_q.start()
            own_q.wait()
            for d in range(1, n_row):
                q_copy(row_peer(d), half).start()

    def gather_owner(o):
        total = jnp.zeros((TILE, cols_dev), jnp.float32)
        for src in range(n_row):
            code = got_labels[src, pl.ds(part_dev, 1), :][:, : part_dev * width]
            spot = lax.broadcasted_iota(jnp.int32, (TILE, part_dev * width), 0) + o * TILE
            onehot = jnp.where(spot == code, 1.0, 0.0).astype(jnp.bfloat16)
            total += lax.dot_general(onehot, wide_hi[src], NN, preferred_element_type=jnp.float32)
            total += lax.dot_general(onehot, wide_lo[src], NN, preferred_element_type=jnp.float32)
        partial[o] = total

    def gather_pair(j, carry):
        gather_owner(2 * j + 1 - parity)
        pair_copy(j).start()
        return carry

    lax.fori_loop(0, pairs, gather_pair, 0)

    def gather_own(j, carry):
        owner = 2 * j + parity
        gather_owner(owner)
        pair_copy(j).wait_recv()
        partial[owner] = partial[owner] + paired[j]

        @pl.when(owner != c)
        def _():
            part_copy(j, place).start()

        return carry

    lax.fori_loop(0, pairs, gather_own, 0)

    own_tile.wait()
    tile_ref[...] = tile_ref[...] - partial[c]

    def collect(d, carry):
        slot = lax.rem(place + pairs - d, pairs)
        part_copy(lax.rem(place + 1, pairs), slot).wait_recv()
        tile_ref[...] = tile_ref[...] - landed[slot]
        return carry

    lax.fori_loop(1, pairs, collect, 0)

    @pl.when(c == 0)
    def _():
        top_ref[...] = tile_ref[:, :PANEL]
        for to in range(1, n_col):
            deal_copy(to).start()

    @pl.when(c != 0)
    def _():
        deal_copy(c).wait_recv()

    for half in range(2):

        @pl.when(r == half)
        def _():
            for d in range(1, n_row):
                lift_copy(row_peer(d), half).start()

    def top_sends(act):
        for d in range(1, n_col):
            to = col_peer(d)

            @pl.when(to != 0)
            def _():
                act(top_copy(to, c))

    top_sends(lambda copy: copy.start())

    for half in range(2):

        @pl.when(r != half)
        def _():
            lift_copy(row_peer(1), half).wait_recv()
            for d in range(1, n_col):
                diag_copy(col_peer(d), half, c).start()

    for half in range(2):

        @pl.when((r == half) & (c == 0))
        def _():
            q_ref[pl.ds(half * TILE, TILE), :] = tile_ref[...]
            for d in range(1, n_row):
                q_rest_copy(row_peer(d), half).start()

    @pl.when(c != 0)
    def _():
        for d in range(1, n_col):
            index = col_peer(d)
            top_copy(index, index).wait_recv()

            @pl.when(index != 0)
            def _():
                raw_copy(index, index).wait_recv()

    for half in range(2):

        @pl.when(r == half)
        def _():
            diag_ref[pl.ds(half * TILE, TILE), :] = top_ref[...]

        @pl.when(r != half)
        def _():
            for d in range(1, n_col):
                index = col_peer(d)
                diag_copy(index, half, index).wait_recv()

        @pl.when((r != half) & (c != 0))
        def _():
            q_copy(row_peer(1), half).wait_recv()

        @pl.when((r != half) & (c == 0))
        def _():
            q_rest_copy(row_peer(1), half).wait_recv()
            q_ref[pl.ds(half * TILE, TILE), :PANEL] = diag_ref[pl.ds(half * TILE, TILE), :]

    for d in range(1, n_row):
        label_copy(row_peer(d), r).wait_send()
        piece_copy(row_peer(d), r).wait_send()

    @pl.when(c == 0)
    def _():
        for to in range(1, n_col):
            raw_deal(to).wait_send()
            deal_copy(to).wait_send()

    @pl.when(c != 0)
    def _():
        for d in range(1, n_col):
            to = col_peer(d)

            @pl.when(to != 0)
            def _():
                raw_copy(to, c).wait_send()

    for j in range(pairs):
        pair_copy(j).wait_send()

        @pl.when(j != place)
        def _():
            part_copy(j, place).wait_send()

    top_sends(lambda copy: copy.wait_send())
    for half in range(2):

        @pl.when(r == half)
        def _():
            for d in range(1, n_row):
                lift_copy(row_peer(d), half).wait_send()

        @pl.when(r != half)
        def _():
            for d in range(1, n_col):
                diag_copy(col_peer(d), half, c).wait_send()

        @pl.when((r == half) & (c != 0))
        def _():
            for d in range(1, n_row):
                q_copy(row_peer(d), half).wait_send()

        @pl.when((r == half) & (c == 0))
        def _():
            for d in range(1, n_row):
                q_rest_copy(row_peer(d), half).wait_send()


def exchange(n_row, n_col, base, pieces, labels):
    rows_dev, cols_dev = base.shape
    part_dev = pieces.shape[1] // (KS // n_row)
    any_spec = pl.BlockSpec(memory_space=pl.ANY)
    vmem_spec = pl.BlockSpec(memory_space=pltpu.VMEM)
    dma = pltpu.SemaphoreType.DMA
    return pl.pallas_call(
        functools.partial(exchange_kernel, n_row, n_col, part_dev),
        out_shape=(
            jax.ShapeDtypeStruct((rows_dev, PANEL), jnp.float32),
            jax.ShapeDtypeStruct((PANEL, cols_dev), jnp.float32),
            jax.ShapeDtypeStruct((PANEL, PANEL), jnp.float32),
            jax.ShapeDtypeStruct((TILE, PANEL), jnp.float32),
            jax.ShapeDtypeStruct((TILE, cols_dev), jnp.float32),
        ),
        in_specs=[any_spec, vmem_spec, vmem_spec],
        out_specs=(any_spec, vmem_spec, vmem_spec, vmem_spec, vmem_spec),
        scratch_shapes=[
            pltpu.VMEM((n_row, KS * part_dev // n_row, KS), jnp.float32),
            pltpu.VMEM(labels.shape, jnp.int32),
            pltpu.VMEM((n_row, KS * part_dev // n_row, cols_dev), jnp.bfloat16),
            pltpu.VMEM((n_row, KS * part_dev // n_row, cols_dev), jnp.bfloat16),
            pltpu.VMEM((n_col, TILE, cols_dev), jnp.float32),
            pltpu.VMEM((n_col // 2, TILE, cols_dev), jnp.float32),
            pltpu.VMEM((n_col // 2, TILE, cols_dev), jnp.float32),
            dma((n_row,)),
            dma((n_row,)),
            dma((n_row,)),
            dma((n_row,)),
            dma((n_col,)),
            dma((n_col,)),
            dma((n_row,)),
            dma((2,)),
            dma((n_col // 2,)),
            dma((n_col // 2,)),
            dma((n_col // 2,)),
            dma((n_col // 2,)),
            dma((n_col,)),
            dma((n_col,)),
            dma((n_col,)),
            dma((n_row,)),
            dma((2,)),
            dma((2, n_col)),
            dma((2, n_col)),
            dma((5,)),
        ],
        compiler_params=pltpu.CompilerParams(
            collective_id=0, has_side_effects=True, vmem_limit_bytes=VMEM_BYTES
        ),
    )(base, pieces, labels)


def full_dot(a, b, dims):
    return lax.dot_general(
        a, b, dims, precision=lax.Precision.HIGHEST, preferred_element_type=jnp.float32
    )


def split_dot(a, b, dims):
    a_high = a.astype(jnp.bfloat16)
    a_low = (a - a_high.astype(jnp.float32)).astype(jnp.bfloat16)
    b_high = b.astype(jnp.bfloat16)
    b_low = (b - b_high.astype(jnp.float32)).astype(jnp.bfloat16)
    dot = functools.partial(
        lax.dot_general, dimension_numbers=dims, preferred_element_type=jnp.float32
    )
    return dot(a_high, b_high) + (dot(a_high, b_low) + dot(a_low, b_high))


STEP = 4


def cholesky_and_inverse(work, block):
    row = lax.broadcasted_iota(jnp.int32, (TILE, TILE), 0)
    col = lax.broadcasted_iota(jnp.int32, (TILE, TILE), 1)
    groups = TILE // 8
    left = block.reshape(groups, 8, TILE)
    right = jnp.where(row == col, 1.0, 0.0).reshape(groups, 8, TILE)
    for k in range(0, TILE, STEP):
        g = k // 8
        s = k % 8
        lanes_left = [
            jnp.broadcast_to(left[0:1, s + i : s + i + 1, :], (1, 8, TILE)) for i in range(STEP)
        ]
        lanes_right = [
            jnp.broadcast_to(right[0:1, s + i : s + i + 1, :], (1, 8, TILE)) for i in range(STEP)
        ]
        cols = [
            jnp.broadcast_to(left[:, :, k + i : k + i + 1], left.shape) for i in range(STEP)
        ]
        heads = [
            [
                jnp.broadcast_to(cols[j][0:1, s + i : s + i + 1, :], (1, 8, TILE))
                for j in range(i + 1)
            ]
            for i in range(STEP)
        ]
        for i in range(STEP):
            scale = lax.rsqrt(heads[i][i])
            lanes_left[i] = lanes_left[i] * scale
            lanes_right[i] = lanes_right[i] * scale
            cols[i] = cols[i] * scale
            below = {}
            for m in range(i + 1, STEP):
                below[m] = heads[m][i] * scale
            for m in range(i + 1, STEP):
                for j in range(i + 1, m + 1):
                    heads[m][j] = heads[m][j] - below[m] * below[j]
                lanes_left[m] = lanes_left[m] - below[m] * lanes_left[i]
                lanes_right[m] = lanes_right[m] - below[m] * lanes_right[i]
                cols[m] = cols[m] - cols[i] * below[m]
        for i in range(STEP):
            work[k + i : k + i + 1, :TILE] = lanes_left[i][0, 0:1, :]
            work[k + i : k + i + 1, TILE:] = lanes_right[i][0, 0:1, :]
        if s + STEP == 8:
            left, right = left[1:], right[1:]
            cols = [x[1:] for x in cols]
        if left.shape[0]:
            for i in range(STEP):
                left = left - cols[i] * lanes_left[i]
                right = right - cols[i] * lanes_right[i]
    upper = jnp.where(row <= col, work[:, :TILE], 0.0)
    inverse = jnp.where(row >= col, work[:, TILE:], 0.0)
    return upper.T, inverse


def factor_kernel(
    base_ref, raw_ref, q_ref, diag_ref, top_ref, tile_ref, out_ref, work, inverse, panel, q_full
):
    r = lax.axis_index("row")
    c = lax.axis_index("col")
    rows_dev, cols_dev = base_ref.shape
    lower0, inverse0 = cholesky_and_inverse(work, diag_ref[:TILE, :TILE])
    lower10 = full_dot(diag_ref[TILE:, :TILE], inverse0, NT)
    lower1, inverse1 = cholesky_and_inverse(
        work, diag_ref[TILE:, TILE:] - full_dot(lower10, lower10, NT)
    )
    inverse[:TILE, :TILE] = inverse0
    inverse[:TILE, TILE:] = jnp.zeros((TILE, TILE), jnp.float32)
    inverse[TILE:, TILE:] = inverse1
    inverse[TILE:, :TILE] = -full_dot(inverse1, full_dot(lower10, inverse0, NN), NN)
    q_full[...] = full_dot(inverse[...], q_ref[...], NN)
    raw_ref[:TILE, :] = top_ref[...]

    def rows(i, carry):
        at = pl.ds(pl.multiple_of(i * TILE, TILE), TILE)
        panel[at, :] = split_dot(raw_ref[at, :], inverse[...], NT)
        return carry

    lax.fori_loop(0, rows_dev // TILE, rows, 0)

    @pl.when(r == 0)
    def _():
        panel[:TILE, :TILE] = lower0
        panel[:TILE, TILE:] = jnp.zeros((TILE, TILE), jnp.float32)

    @pl.when(r == 1)
    def _():
        panel[:TILE, :TILE] = lower10
        panel[:TILE, TILE:] = lower1

    def trailing(i, carry):
        at = pl.ds(pl.multiple_of(i * TILE, TILE), TILE)
        current = jnp.where(i == c, tile_ref[...], base_ref[at, :])
        out_ref[at, :] = current - split_dot(panel[at, :], q_full[...], NN)
        return carry

    lax.fori_loop(0, rows_dev // TILE, trailing, 0)

    @pl.when(r < 2)
    def _():
        out_ref[:TILE, :] = jnp.zeros((TILE, cols_dev), jnp.float32)

    @pl.when(c == 0)
    def _():
        out_ref[:, :PANEL] = panel[...]


def factorise(base, raw, q, diag, top, tile):
    rows_dev, cols_dev = base.shape
    vmem_spec = pl.BlockSpec(memory_space=pltpu.VMEM)
    return pl.pallas_call(
        factor_kernel,
        out_shape=jax.ShapeDtypeStruct(base.shape, jnp.float32),
        in_specs=[vmem_spec] * 6,
        out_specs=vmem_spec,
        scratch_shapes=[
            pltpu.VMEM((TILE, 2 * TILE), jnp.float32),
            pltpu.VMEM((PANEL, PANEL), jnp.float32),
            pltpu.VMEM((rows_dev, PANEL), jnp.float32),
            pltpu.VMEM((PANEL, cols_dev), jnp.float32),
        ],
        compiler_params=pltpu.CompilerParams(vmem_limit_bytes=VMEM_BYTES),
    )(base, raw, q, diag, top, tile)


def local(base_matrix, inverse_factors, coupling, positions, counts, owners):
    n_row = lax.axis_size("row")
    n_col = lax.axis_size("col")
    part_dev = coupling.shape[0]
    width = KS // n_row
    factor = jnp.einsum(
        "pbij,pbjk->pbik", inverse_factors, coupling, preferred_element_type=jnp.float32
    ).astype(jnp.bfloat16)
    schur_rows = jnp.einsum("pbik,pbil->pkl", factor, factor, preferred_element_type=jnp.float32)
    pieces = schur_rows.reshape(part_dev, n_row, width, KS).transpose(1, 0, 2, 3)
    pieces = pieces.reshape(n_row, part_dev * width, KS)
    within = jnp.arange(width, dtype=jnp.int32)
    group = jnp.arange(n_row, dtype=jnp.int32)
    usable = within[None, None, :] < counts[:, :, None]
    place = positions.reshape(part_dev, n_row, width)
    col_code = jnp.where(usable, group[None, :, None] * TILE + place, -1).reshape(part_dev, KS)
    row_code = jnp.where(usable, owners[:, None, None] * TILE + place, -1)
    row_code = row_code.transpose(1, 0, 2).reshape(n_row, 1, part_dev * width)
    labels = jnp.concatenate(
        [
            jnp.broadcast_to(col_code[None], (n_row, part_dev, KS)),
            jnp.pad(row_code, ((0, 0), (0, 0), (0, KS - part_dev * width))),
            jnp.zeros((n_row, 7 - part_dev, KS), jnp.int32),
        ],
        axis=1,
    )
    raw, q, diag, top, tile = exchange(n_row, n_col, base_matrix, pieces, labels)
    return factorise(base_matrix, raw, q, diag, top, tile)


def solution(mesh):
    in_specs = (
        P("row", "col"),
        P(("row", "col"), None, None, None),
        P(("row", "col"), None, None, None),
        P(("row", "col"), None),
        P(("row", "col"), None),
        P(("row", "col")),
    )
    out_specs = P("row", "col")
    return jax.shard_map(local, mesh=mesh, in_specs=in_specs, out_specs=out_specs, check_vma=False)
```

```python
import functools

import jax
import jax.numpy as jnp
from jax import lax
from jax.experimental import pallas as pl
from jax.experimental.pallas import tpu as pltpu
from jax.sharding import PartitionSpec as P

TILE = 128
KS = 256
PANEL = 2 * TILE
VMEM_BYTES = 50 * 1024 * 1024
MESH = pl.DeviceIdType.MESH
NT = (((1,), (1,)), ((), ()))
NN = (((1,), (0,)), ((), ()))
TN = (((0,), (0,)), ((), ()))


def exchange_kernel(
    n_row,
    n_col,
    part_dev,
    base_ref,
    factors_ref,
    coupling_ref,
    positions_ref,
    counts_ref,
    owners_ref,
    raw_ref,
    q_ref,
    diag_ref,
    top_ref,
    tile_ref,
    factors,
    couplings,
    pieces,
    labels,
    got,
    got_labels,
    wide_hi,
    wide_lo,
    partial,
    paired,
    landed,
    piece_send,
    piece_recv,
    label_send,
    label_recv,
    raw_send,
    raw_recv,
    q_send,
    q_recv,
    pair_send,
    pair_recv,
    part_send,
    part_recv,
    deal_send,
    top_send,
    top_recv,
    lift_send,
    lift_recv,
    diag_send,
    diag_recv,
    local_sem,
    load_sem,
):
    r = lax.axis_index("row")
    c = lax.axis_index("col")
    width = KS // n_row
    cols_dev = n_row * TILE
    chunk = TILE // n_col
    parity = lax.rem(c, 2)
    twin = c + 1 - 2 * parity
    pairs = n_col // 2
    place = lax.div(c, 2)

    def row_peer(d):
        return lax.rem(r + d, n_row)

    def col_peer(d):
        return lax.rem(c + d, n_col)

    def send(src, dst, send_sem, recv_sem, axis, to):
        return pltpu.make_async_remote_copy(
            src_ref=src,
            dst_ref=dst,
            send_sem=send_sem,
            recv_sem=recv_sem,
            device_id={axis: to},
            device_id_type=MESH,
        )

    def piece_copy(to, slot, p):
        at = pl.ds(p * width, width)
        return send(
            pieces.at[to, at], got.at[slot, at], piece_send.at[to, p], piece_recv.at[slot, p], "row", to
        )

    def label_copy(to, slot):
        return send(
            labels.at[to], got_labels.at[slot], label_send.at[to], label_recv.at[slot], "row", to
        )

    def raw_deal(to):
        at = pl.ds(to * TILE, TILE)
        return send(
            base_ref.at[at, pl.ds(0, PANEL)],
            raw_ref.at[at],
            raw_send.at[to],
            raw_recv.at[to],
            "col",
            to,
        )

    def raw_copy(to, index):
        at = pl.ds(index * TILE, TILE)
        return send(
            raw_ref.at[at], raw_ref.at[at], raw_send.at[to], raw_recv.at[index], "col", to
        )

    def q_copy(to, half):
        at = pl.ds(half * TILE, TILE)
        return send(q_ref.at[at], q_ref.at[at], q_send.at[half, to], q_recv.at[half], "row", to)

    def q_rest_copy(to, half):
        at = q_ref.at[pl.ds(half * TILE, TILE), pl.ds(PANEL, cols_dev - PANEL)]
        return send(at, at, q_send.at[half, to], q_recv.at[half], "row", to)

    def pair_copy(j):
        owner = 2 * j + 1 - parity
        return send(partial.at[owner], paired.at[j], pair_send.at[j], pair_recv.at[j], "col", twin)

    def part_copy(j, slot):
        owner = 2 * j + parity
        return send(
            partial.at[owner], landed.at[slot], part_send.at[j], part_recv.at[slot], "col", owner
        )

    def deal_copy(to):
        at = top_ref.at[pl.ds(to * chunk, chunk)]
        return send(at, at, deal_send.at[to], top_recv.at[to], "col", to)

    def top_copy(to, index):
        at = top_ref.at[pl.ds(index * chunk, chunk)]
        return send(at, at, top_send.at[to], top_recv.at[index], "col", to)

    def lift_copy(to, half):
        return send(
            top_ref.at[pl.ds(c * chunk, chunk)],
            diag_ref.at[pl.ds(half * TILE + c * chunk, chunk)],
            lift_send.at[to],
            lift_recv.at[half],
            "row",
            to,
        )

    def diag_copy(to, half, index):
        at = diag_ref.at[pl.ds(half * TILE + index * chunk, chunk)]
        return send(at, at, diag_send.at[half, to], diag_recv.at[half, index], "col", to)

    def load(p, part):
        src, dst = ((factors_ref, factors), (coupling_ref, couplings))[part]
        return pltpu.make_async_copy(src.at[p], dst.at[p], load_sem.at[part, p])

    for p in range(part_dev):
        load(p, 0).start()
        load(p, 1).start()

    barrier = pltpu.get_barrier_semaphore()
    for d in range(1, n_row):
        pl.semaphore_signal(barrier, inc=1, device_id={"row": row_peer(d)}, device_id_type=MESH)
    for d in range(1, n_col):
        pl.semaphore_signal(barrier, inc=1, device_id={"col": col_peer(d)}, device_id_type=MESH)

    lane = lax.broadcasted_iota(jnp.int32, (1, KS), 1)
    places = positions_ref[...]
    usable, columns = [], []
    for p in range(part_dev):
        limit = jnp.zeros((1, KS), jnp.int32)
        offset = jnp.zeros((1, KS), jnp.int32)
        for g in range(n_row):
            inside = (lane >= g * width) & (lane < (g + 1) * width)
            limit = jnp.where(inside, counts_ref[p, g] + g * width, limit)
            offset = jnp.where(inside, g * TILE, offset)
        used = lane < limit
        columns.append(jnp.where(used, places[p : p + 1, :] + offset, -1))
        usable.append(jnp.where(used, places[p : p + 1, :] + owners_ref[p] * TILE, -1))
    column_codes = jnp.concatenate(columns, axis=0)
    for g in range(n_row):
        labels[g, :part_dev, :] = column_codes
        labels[g, part_dev : part_dev + 1, : part_dev * width] = jnp.concatenate(
            [x[:, g * width : (g + 1) * width] for x in usable], axis=1
        )

    pl.semaphore_wait(barrier, n_row + n_col - 2)

    for d in range(1, n_row):
        label_copy(row_peer(d), r).start()
    own_label = pltpu.make_async_copy(labels.at[r], got_labels.at[r], local_sem.at[1])
    own_label.start()
    own_tile = pltpu.make_async_copy(
        base_ref.at[pl.ds(c * TILE, TILE)], tile_ref, local_sem.at[3]
    )
    own_tile.start()

    @pl.when(c == 0)
    def _():
        for to in range(1, n_col):
            raw_deal(to).start()
        own_raw = pltpu.make_async_copy(
            base_ref.at[:, pl.ds(0, PANEL)], raw_ref, local_sem.at[2]
        )
        own_raw.start()
        own_raw.wait()

    for p in range(part_dev):
        load(p, 0).wait()
        load(p, 1).wait()
        schur = jnp.zeros((KS, KS), jnp.float32)
        for b in range(factors_ref.shape[1]):
            factor = jnp.dot(
                factors[p, b], couplings[p, b], preferred_element_type=jnp.float32
            ).astype(jnp.bfloat16)
            schur += lax.dot_general(factor, factor, TN, preferred_element_type=jnp.float32)
        for g in range(n_row):
            pieces[g, pl.ds(p * width, width), :] = schur[g * width : (g + 1) * width, :]
        for d in range(1, n_row):
            piece_copy(row_peer(d), r, p).start()

    own_piece = pltpu.make_async_copy(pieces.at[r], got.at[r], local_sem.at[0])
    own_piece.start()
    own_piece.wait()
    own_label.wait()

    def widen(src):
        for p in range(part_dev):
            block = got[src, pl.ds(p * width, width), :]
            high = block.astype(jnp.bfloat16)
            low = (block - high.astype(jnp.float32)).astype(jnp.bfloat16)
            code = got_labels[src, pl.ds(p, 1), :]
            spot = lax.broadcasted_iota(jnp.int32, (cols_dev, KS), 0)
            onehot = jnp.where(spot == code, 1.0, 0.0).astype(jnp.bfloat16)
            both = jnp.concatenate([high, low], axis=0)
            out = lax.dot_general(both, onehot, NT, preferred_element_type=jnp.float32)
            out = out.astype(jnp.bfloat16)
            wide_hi[src, pl.ds(p * width, width), :] = out[:width]
            wide_lo[src, pl.ds(p * width, width), :] = out[width:]

    widen(r)

    @pl.when(c != 0)
    def _():
        raw_copy(0, c).wait_recv()
        for d in range(1, n_col):
            to = col_peer(d)

            @pl.when(to != 0)
            def _():
                raw_copy(to, c).start()

    def arrive(d, carry):
        src = lax.rem(r + n_row - d, n_row)
        label_copy(row_peer(1), src).wait_recv()
        for p in range(part_dev):
            piece_copy(row_peer(1), src, p).wait_recv()
        widen(src)
        return carry

    lax.fori_loop(1, n_row, arrive, 0)

    def q_out(make, half, act):
        if half > 0:
            act(make(half - 1, half))
        act(make(half + 1, half))

    def q_forward(make, half, first, last):
        @pl.when((r > half) & (r >= first) & (r < last))
        def _():
            make(r + 1, half).wait_recv()
            make(r + 1, half).start()

    for half in range(2):

        @pl.when((r == half) & (c != 0))
        def _():
            own_q = pltpu.make_async_copy(
                base_ref.at[pl.ds(0, TILE)], q_ref.at[pl.ds(half * TILE, TILE)], local_sem.at[4]
            )
            own_q.start()
            own_q.wait()
            q_out(q_copy, half, lambda copy: copy.start())

    def gather_owner(o):
        total = jnp.zeros((TILE, cols_dev), jnp.float32)
        for src in range(n_row):
            code = got_labels[src, pl.ds(part_dev, 1), :][:, : part_dev * width]
            spot = lax.broadcasted_iota(jnp.int32, (TILE, part_dev * width), 0) + o * TILE
            onehot = jnp.where(spot == code, 1.0, 0.0).astype(jnp.bfloat16)
            total += lax.dot_general(onehot, wide_hi[src], NN, preferred_element_type=jnp.float32)
            total += lax.dot_general(onehot, wide_lo[src], NN, preferred_element_type=jnp.float32)
        partial[o] = total

    def gather_pair(j, carry):
        gather_owner(2 * j + 1 - parity)
        pair_copy(j).start()
        return carry

    lax.fori_loop(0, pairs, gather_pair, 0)

    @pl.when(c != 0)
    def _():
        for half in range(2):
            q_forward(q_copy, half, 0, 2)

    def gather_own(j, carry):
        owner = 2 * j + parity
        gather_owner(owner)
        pair_copy(j).wait_recv()
        partial[owner] = partial[owner] + paired[j]

        @pl.when(owner != c)
        def _():
            part_copy(j, place).start()

        return carry

    lax.fori_loop(0, pairs, gather_own, 0)

    own_tile.wait()
    tile_ref[...] = tile_ref[...] - partial[c]

    def collect(d, carry):
        slot = lax.rem(place + pairs - d, pairs)
        part_copy(lax.rem(place + 1, pairs), slot).wait_recv()
        tile_ref[...] = tile_ref[...] - landed[slot]
        return carry

    lax.fori_loop(1, pairs, collect, 0)

    @pl.when(c == 0)
    def _():
        top_ref[...] = tile_ref[:, :PANEL]
        for to in range(1, n_col):
            deal_copy(to).start()

    @pl.when(c != 0)
    def _():
        deal_copy(c).wait_recv()

    for half in range(2):

        @pl.when(r == half)
        def _():
            for d in range(1, n_row):
                lift_copy(row_peer(d), half).start()

    def top_sends(act):
        for d in range(1, n_col):
            to = col_peer(d)

            @pl.when(to != 0)
            def _():
                act(top_copy(to, c))

    top_sends(lambda copy: copy.start())

    for half in range(2):

        @pl.when(r != half)
        def _():
            lift_copy(row_peer(1), half).wait_recv()
            for d in range(1, n_col):
                diag_copy(col_peer(d), half, c).start()

    for half in range(2):

        @pl.when((r == half) & (c == 0))
        def _():
            q_ref[pl.ds(half * TILE, TILE), :] = tile_ref[...]
            q_out(q_rest_copy, half, lambda copy: copy.start())

    for half in range(2):

        @pl.when(c != 0)
        def _():
            q_forward(q_copy, half, 2, n_row - 1)

        @pl.when(c == 0)
        def _():
            q_forward(q_rest_copy, half, 0, n_row - 1)

    @pl.when(c != 0)
    def _():
        for d in range(1, n_col):
            index = col_peer(d)
            top_copy(index, index).wait_recv()

            @pl.when(index != 0)
            def _():
                raw_copy(index, index).wait_recv()

    for half in range(2):

        @pl.when(r == half)
        def _():
            diag_ref[pl.ds(half * TILE, TILE), :] = top_ref[...]

        @pl.when(r != half)
        def _():
            for d in range(1, n_col):
                index = col_peer(d)
                diag_copy(index, half, index).wait_recv()

        @pl.when(((r < half) | (r == n_row - 1)) & (c != 0))
        def _():
            q_copy(row_peer(1), half).wait_recv()

        @pl.when(((r < half) | (r == n_row - 1)) & (c == 0))
        def _():
            q_rest_copy(row_peer(1), half).wait_recv()

        @pl.when((r != half) & (c == 0))
        def _():
            q_ref[pl.ds(half * TILE, TILE), :PANEL] = diag_ref[pl.ds(half * TILE, TILE), :]

    for d in range(1, n_row):
        label_copy(row_peer(d), r).wait_send()
        for p in range(part_dev):
            piece_copy(row_peer(d), r, p).wait_send()

    @pl.when(c == 0)
    def _():
        for to in range(1, n_col):
            raw_deal(to).wait_send()
            deal_copy(to).wait_send()

    @pl.when(c != 0)
    def _():
        for d in range(1, n_col):
            to = col_peer(d)

            @pl.when(to != 0)
            def _():
                raw_copy(to, c).wait_send()

    for j in range(pairs):
        pair_copy(j).wait_send()

        @pl.when(j != place)
        def _():
            part_copy(j, place).wait_send()

    top_sends(lambda copy: copy.wait_send())
    for half in range(2):

        @pl.when(r == half)
        def _():
            for d in range(1, n_row):
                lift_copy(row_peer(d), half).wait_send()

        @pl.when(r != half)
        def _():
            for d in range(1, n_col):
                diag_copy(col_peer(d), half, c).wait_send()

        @pl.when((r == half) & (c != 0))
        def _():
            q_out(q_copy, half, lambda copy: copy.wait_send())

        @pl.when((r > half) & (r < n_row - 1) & (c != 0))
        def _():
            q_copy(r + 1, half).wait_send()

        @pl.when((r == half) & (c == 0))
        def _():
            q_out(q_rest_copy, half, lambda copy: copy.wait_send())

        @pl.when((r > half) & (r < n_row - 1) & (c == 0))
        def _():
            q_rest_copy(r + 1, half).wait_send()


def exchange(n_row, n_col, base, factors, coupling, positions, counts, owners):
    rows_dev, cols_dev = base.shape
    part_dev = coupling.shape[0]
    smem_spec = pl.BlockSpec(memory_space=pltpu.SMEM)
    any_spec = pl.BlockSpec(memory_space=pl.ANY)
    vmem_spec = pl.BlockSpec(memory_space=pltpu.VMEM)
    dma = pltpu.SemaphoreType.DMA
    return pl.pallas_call(
        functools.partial(exchange_kernel, n_row, n_col, part_dev),
        out_shape=(
            jax.ShapeDtypeStruct((rows_dev, PANEL), jnp.float32),
            jax.ShapeDtypeStruct((PANEL, cols_dev), jnp.float32),
            jax.ShapeDtypeStruct((PANEL, PANEL), jnp.float32),
            jax.ShapeDtypeStruct((TILE, PANEL), jnp.float32),
            jax.ShapeDtypeStruct((TILE, cols_dev), jnp.float32),
        ),
        in_specs=[any_spec, any_spec, any_spec, vmem_spec, smem_spec, smem_spec],
        out_specs=(any_spec, vmem_spec, vmem_spec, vmem_spec, vmem_spec),
        scratch_shapes=[
            pltpu.VMEM(factors.shape, factors.dtype),
            pltpu.VMEM(coupling.shape, coupling.dtype),
            pltpu.VMEM((n_row, KS * part_dev // n_row, KS), jnp.float32),
            pltpu.VMEM((n_row, 8, KS), jnp.int32),
            pltpu.VMEM((n_row, KS * part_dev // n_row, KS), jnp.float32),
            pltpu.VMEM((n_row, 8, KS), jnp.int32),
            pltpu.VMEM((n_row, KS * part_dev // n_row, cols_dev), jnp.bfloat16),
            pltpu.VMEM((n_row, KS * part_dev // n_row, cols_dev), jnp.bfloat16),
            pltpu.VMEM((n_col, TILE, cols_dev), jnp.float32),
            pltpu.VMEM((n_col // 2, TILE, cols_dev), jnp.float32),
            pltpu.VMEM((n_col // 2, TILE, cols_dev), jnp.float32),
            dma((n_row, part_dev)),
            dma((n_row, part_dev)),
            dma((n_row,)),
            dma((n_row,)),
            dma((n_col,)),
            dma((n_col,)),
            dma((2, n_row)),
            dma((2,)),
            dma((n_col // 2,)),
            dma((n_col // 2,)),
            dma((n_col // 2,)),
            dma((n_col // 2,)),
            dma((n_col,)),
            dma((n_col,)),
            dma((n_col,)),
            dma((n_row,)),
            dma((2,)),
            dma((2, n_col)),
            dma((2, n_col)),
            dma((5,)),
            dma((2, part_dev)),
        ],
        compiler_params=pltpu.CompilerParams(
            collective_id=0, has_side_effects=True, vmem_limit_bytes=VMEM_BYTES
        ),
    )(base, factors, coupling, positions, counts, owners)


def full_dot(a, b, dims):
    return lax.dot_general(
        a, b, dims, precision=lax.Precision.HIGHEST, preferred_element_type=jnp.float32
    )


def split_dot(a, b, dims):
    a_high = a.astype(jnp.bfloat16)
    a_low = (a - a_high.astype(jnp.float32)).astype(jnp.bfloat16)
    b_high = b.astype(jnp.bfloat16)
    b_low = (b - b_high.astype(jnp.float32)).astype(jnp.bfloat16)
    dot = functools.partial(
        lax.dot_general, dimension_numbers=dims, preferred_element_type=jnp.float32
    )
    return dot(a_high, b_high) + (dot(a_high, b_low) + dot(a_low, b_high))


STEP = 8


def cholesky_and_inverse(work, block):
    row = lax.broadcasted_iota(jnp.int32, (TILE, TILE), 0)
    col = lax.broadcasted_iota(jnp.int32, (TILE, TILE), 1)
    groups = TILE // 8
    left = block.reshape(groups, 8, TILE)
    right = jnp.where(row == col, 1.0, 0.0).reshape(groups, 8, TILE)
    for k in range(0, TILE, STEP):
        g = k // 8
        s = k % 8
        lanes_left = [
            jnp.broadcast_to(left[0:1, s + i : s + i + 1, :], (1, 8, TILE)) for i in range(STEP)
        ]
        lanes_right = [
            jnp.broadcast_to(right[0:1, s + i : s + i + 1, :], (1, 8, TILE)) for i in range(STEP)
        ]
        cols = [
            jnp.broadcast_to(left[:, :, k + i : k + i + 1], left.shape) for i in range(STEP)
        ]
        heads = [
            [
                jnp.broadcast_to(cols[j][0:1, s + i : s + i + 1, :], (1, 8, TILE))
                for j in range(i + 1)
            ]
            for i in range(STEP)
        ]
        for i in range(STEP):
            scale = lax.rsqrt(heads[i][i])
            lanes_left[i] = lanes_left[i] * scale
            lanes_right[i] = lanes_right[i] * scale
            cols[i] = cols[i] * scale
            below = {}
            for m in range(i + 1, STEP):
                below[m] = heads[m][i] * scale
            for m in range(i + 1, STEP):
                for j in range(i + 1, m + 1):
                    heads[m][j] = heads[m][j] - below[m] * below[j]
                lanes_left[m] = lanes_left[m] - below[m] * lanes_left[i]
                lanes_right[m] = lanes_right[m] - below[m] * lanes_right[i]
                cols[m] = cols[m] - cols[i] * below[m]
        for i in range(STEP):
            work[k + i : k + i + 1, :TILE] = lanes_left[i][0, 0:1, :]
            work[k + i : k + i + 1, TILE:] = lanes_right[i][0, 0:1, :]
        if s + STEP == 8:
            left, right = left[1:], right[1:]
            cols = [x[1:] for x in cols]
        if left.shape[0]:
            for i in range(STEP):
                left = left - cols[i] * lanes_left[i]
                right = right - cols[i] * lanes_right[i]
    upper = jnp.where(row <= col, work[:, :TILE], 0.0)
    inverse = jnp.where(row >= col, work[:, TILE:], 0.0)
    return upper.T, inverse


def factor_kernel(
    base_ref, raw_ref, q_ref, diag_ref, top_ref, tile_ref, out_ref, work, inverse, panel, q_full
):
    r = lax.axis_index("row")
    c = lax.axis_index("col")
    rows_dev, cols_dev = base_ref.shape
    lower0, inverse0 = cholesky_and_inverse(work, diag_ref[:TILE, :TILE])
    lower10 = full_dot(diag_ref[TILE:, :TILE], inverse0, NT)
    lower1, inverse1 = cholesky_and_inverse(
        work, diag_ref[TILE:, TILE:] - full_dot(lower10, lower10, NT)
    )
    inverse[:TILE, :TILE] = inverse0
    inverse[:TILE, TILE:] = jnp.zeros((TILE, TILE), jnp.float32)
    inverse[TILE:, TILE:] = inverse1
    inverse[TILE:, :TILE] = -full_dot(inverse1, full_dot(lower10, inverse0, NN), NN)
    q_full[...] = full_dot(inverse[...], q_ref[...], NN)
    raw_ref[:TILE, :] = top_ref[...]

    def rows(i, carry):
        at = pl.ds(pl.multiple_of(i * TILE, TILE), TILE)
        panel[at, :] = split_dot(raw_ref[at, :], inverse[...], NT)
        return carry

    lax.fori_loop(0, rows_dev // TILE, rows, 0)

    @pl.when(r == 0)
    def _():
        panel[:TILE, :TILE] = lower0
        panel[:TILE, TILE:] = jnp.zeros((TILE, TILE), jnp.float32)

    @pl.when(r == 1)
    def _():
        panel[:TILE, :TILE] = lower10
        panel[:TILE, TILE:] = lower1

    def trailing(i, carry):
        at = pl.ds(pl.multiple_of(i * TILE, TILE), TILE)
        current = jnp.where(i == c, tile_ref[...], base_ref[at, :])
        out_ref[at, :] = current - split_dot(panel[at, :], q_full[...], NN)
        return carry

    lax.fori_loop(0, rows_dev // TILE, trailing, 0)

    @pl.when(r < 2)
    def _():
        out_ref[:TILE, :] = jnp.zeros((TILE, cols_dev), jnp.float32)

    @pl.when(c == 0)
    def _():
        out_ref[:, :PANEL] = panel[...]


def factorise(base, raw, q, diag, top, tile):
    rows_dev, cols_dev = base.shape
    vmem_spec = pl.BlockSpec(memory_space=pltpu.VMEM)
    return pl.pallas_call(
        factor_kernel,
        out_shape=jax.ShapeDtypeStruct(base.shape, jnp.float32),
        in_specs=[vmem_spec] * 6,
        out_specs=vmem_spec,
        scratch_shapes=[
            pltpu.VMEM((TILE, 2 * TILE), jnp.float32),
            pltpu.VMEM((PANEL, PANEL), jnp.float32),
            pltpu.VMEM((rows_dev, PANEL), jnp.float32),
            pltpu.VMEM((PANEL, cols_dev), jnp.float32),
        ],
        compiler_params=pltpu.CompilerParams(vmem_limit_bytes=VMEM_BYTES),
    )(base, raw, q, diag, top, tile)


def local(base_matrix, inverse_factors, coupling, positions, counts, owners):
    n_row = lax.axis_size("row")
    n_col = lax.axis_size("col")
    raw, q, diag, top, tile = exchange(
        n_row, n_col, base_matrix, inverse_factors, coupling, positions, counts, owners
    )
    return factorise(base_matrix, raw, q, diag, top, tile)


def solution(mesh):
    in_specs = (
        P("row", "col"),
        P(("row", "col"), None, None, None),
        P(("row", "col"), None, None, None),
        P(("row", "col"), None),
        P(("row", "col"), None),
        P(("row", "col")),
    )
    out_specs = P("row", "col")
    return jax.shard_map(local, mesh=mesh, in_specs=in_specs, out_specs=out_specs, check_vma=False)
```

```python
import functools

import jax
import jax.numpy as jnp
from jax import lax
from jax.experimental import pallas as pl
from jax.experimental.pallas import tpu as pltpu
from jax.sharding import PartitionSpec as P

TILE = 128
KS = 256
PANEL = 2 * TILE
VMEM_BYTES = 50 * 1024 * 1024
MESH = pl.DeviceIdType.MESH
NT = (((1,), (1,)), ((), ()))
NN = (((1,), (0,)), ((), ()))
TN = (((0,), (0,)), ((), ()))


def exchange_kernel(
    n_row,
    n_col,
    part_dev,
    base_ref,
    factors_ref,
    coupling_ref,
    positions_ref,
    counts_ref,
    owners_ref,
    raw_ref,
    q_ref,
    diag_ref,
    top_ref,
    tile_ref,
    factors,
    couplings,
    pieces,
    labels,
    got,
    got_labels,
    wide_hi,
    wide_lo,
    partial,
    paired,
    landed,
    piece_send,
    piece_recv,
    label_send,
    label_recv,
    raw_send,
    raw_recv,
    q_send,
    q_recv,
    pair_send,
    pair_recv,
    part_send,
    part_recv,
    deal_send,
    top_send,
    top_recv,
    lift_send,
    lift_recv,
    diag_send,
    diag_recv,
    local_sem,
    load_sem,
):
    r = lax.axis_index("row")
    c = lax.axis_index("col")
    width = KS // n_row
    cols_dev = n_row * TILE
    chunk = TILE // n_col
    parity = lax.rem(c, 2)
    twin = c + 1 - 2 * parity
    pairs = n_col // 2
    place = lax.div(c, 2)

    def row_peer(d):
        return lax.rem(r + d, n_row)

    def col_peer(d):
        return lax.rem(c + d, n_col)

    def send(src, dst, send_sem, recv_sem, axis, to):
        return pltpu.make_async_remote_copy(
            src_ref=src,
            dst_ref=dst,
            send_sem=send_sem,
            recv_sem=recv_sem,
            device_id={axis: to},
            device_id_type=MESH,
        )

    def piece_copy(to, slot, p):
        at = pl.ds(p * width, width)
        return send(
            pieces.at[to, at], got.at[slot, at], piece_send.at[to, p], piece_recv.at[slot, p], "row", to
        )

    def label_copy(to, slot):
        return send(
            labels.at[to], got_labels.at[slot], label_send.at[to], label_recv.at[slot], "row", to
        )

    def raw_deal(to):
        at = pl.ds(to * TILE, TILE)
        return send(
            base_ref.at[at, pl.ds(0, PANEL)],
            raw_ref.at[at],
            raw_send.at[to],
            raw_recv.at[to],
            "col",
            to,
        )

    def raw_copy(to, index):
        at = pl.ds(index * TILE, TILE)
        return send(
            raw_ref.at[at], raw_ref.at[at], raw_send.at[to], raw_recv.at[index], "col", to
        )

    def q_copy(to, half):
        at = pl.ds(half * TILE, TILE)
        return send(q_ref.at[at], q_ref.at[at], q_send.at[half, to], q_recv.at[half], "row", to)

    def q_rest_copy(to, half):
        at = q_ref.at[pl.ds(half * TILE, TILE), pl.ds(PANEL, cols_dev - PANEL)]
        return send(at, at, q_send.at[half, to], q_recv.at[half], "row", to)

    def pair_copy(j):
        owner = 2 * j + 1 - parity
        return send(partial.at[owner], paired.at[j], pair_send.at[j], pair_recv.at[j], "col", twin)

    def part_copy(j, slot):
        owner = 2 * j + parity
        return send(
            partial.at[owner], landed.at[slot], part_send.at[j], part_recv.at[slot], "col", owner
        )

    def deal_copy(to):
        at = top_ref.at[pl.ds(to * chunk, chunk)]
        return send(at, at, deal_send.at[to], top_recv.at[to], "col", to)

    def top_copy(to, index):
        at = top_ref.at[pl.ds(index * chunk, chunk)]
        return send(at, at, top_send.at[to], top_recv.at[index], "col", to)

    def lift_copy(to, half):
        return send(
            top_ref.at[pl.ds(c * chunk, chunk)],
            diag_ref.at[pl.ds(half * TILE + c * chunk, chunk)],
            lift_send.at[to],
            lift_recv.at[half],
            "row",
            to,
        )

    def diag_copy(to, half, index):
        at = diag_ref.at[pl.ds(half * TILE + index * chunk, chunk)]
        return send(at, at, diag_send.at[half, to], diag_recv.at[half, index], "col", to)

    def load(p, part):
        src, dst = ((factors_ref, factors), (coupling_ref, couplings))[part]
        return pltpu.make_async_copy(src.at[p], dst.at[p], load_sem.at[part, p])

    for p in range(part_dev):
        load(p, 0).start()
        load(p, 1).start()

    barrier = pltpu.get_barrier_semaphore()
    for d in range(1, n_row):
        pl.semaphore_signal(barrier, inc=1, device_id={"row": row_peer(d)}, device_id_type=MESH)
    for d in range(1, n_col):
        pl.semaphore_signal(barrier, inc=1, device_id={"col": col_peer(d)}, device_id_type=MESH)

    lane = lax.broadcasted_iota(jnp.int32, (1, KS), 1)
    places = positions_ref[...]
    usable, columns = [], []
    for p in range(part_dev):
        limit = jnp.zeros((1, KS), jnp.int32)
        offset = jnp.zeros((1, KS), jnp.int32)
        for g in range(n_row):
            inside = (lane >= g * width) & (lane < (g + 1) * width)
            limit = jnp.where(inside, counts_ref[p, g] + g * width, limit)
            offset = jnp.where(inside, g * TILE, offset)
        used = lane < limit
        columns.append(jnp.where(used, places[p : p + 1, :] + offset, -1))
        usable.append(jnp.where(used, places[p : p + 1, :] + owners_ref[p] * TILE, -1))
    column_codes = jnp.concatenate(columns, axis=0)
    for g in range(n_row):
        labels[g, :part_dev, :] = column_codes
        labels[g, part_dev : part_dev + 1, : part_dev * width] = jnp.concatenate(
            [x[:, g * width : (g + 1) * width] for x in usable], axis=1
        )

    pl.semaphore_wait(barrier, n_row + n_col - 2)

    for d in range(1, n_row):
        label_copy(row_peer(d), r).start()
    own_label = pltpu.make_async_copy(labels.at[r], got_labels.at[r], local_sem.at[1])
    own_label.start()
    def q_out(make, half, act):
        if half > 0:
            act(make(half - 1, half))
        act(make(half + 1, half))

    def q_forward(make, half, first, last):
        @pl.when((r > half) & (r >= first) & (r < last))
        def _():
            make(r + 1, half).wait_recv()
            make(r + 1, half).start()

    for half in range(2):

        @pl.when((r == half) & (c != 0))
        def _():
            own_q = pltpu.make_async_copy(
                base_ref.at[pl.ds(0, TILE)], q_ref.at[pl.ds(half * TILE, TILE)], local_sem.at[4]
            )
            own_q.start()
            own_q.wait()
            q_out(q_copy, half, lambda copy: copy.start())

    own_tile = pltpu.make_async_copy(
        base_ref.at[pl.ds(c * TILE, TILE)], tile_ref, local_sem.at[3]
    )
    own_tile.start()

    @pl.when(c == 0)
    def _():
        for to in range(1, n_col):
            raw_deal(to).start()
        own_raw = pltpu.make_async_copy(
            base_ref.at[:, pl.ds(0, PANEL)], raw_ref, local_sem.at[2]
        )
        own_raw.start()
        own_raw.wait()

    for p in range(part_dev):
        load(p, 0).wait()
        load(p, 1).wait()
        schur = jnp.zeros((KS, KS), jnp.float32)
        for b in range(factors_ref.shape[1]):
            factor = jnp.dot(
                factors[p, b], couplings[p, b], preferred_element_type=jnp.float32
            ).astype(jnp.bfloat16)
            schur += lax.dot_general(factor, factor, TN, preferred_element_type=jnp.float32)
        for g in range(n_row):
            pieces[g, pl.ds(p * width, width), :] = schur[g * width : (g + 1) * width, :]
        for d in range(1, n_row):
            piece_copy(row_peer(d), r, p).start()

    @pl.when(c != 0)
    def _():
        for half in range(2):
            q_forward(q_copy, half, 0, 2)

    own_piece = pltpu.make_async_copy(pieces.at[r], got.at[r], local_sem.at[0])
    own_piece.start()
    own_piece.wait()
    own_label.wait()

    def widen(src):
        for p in range(part_dev):
            block = got[src, pl.ds(p * width, width), :]
            high = block.astype(jnp.bfloat16)
            low = (block - high.astype(jnp.float32)).astype(jnp.bfloat16)
            code = got_labels[src, pl.ds(p, 1), :]
            spot = lax.broadcasted_iota(jnp.int32, (cols_dev, KS), 0)
            onehot = jnp.where(spot == code, 1.0, 0.0).astype(jnp.bfloat16)
            both = jnp.concatenate([high, low], axis=0)
            out = lax.dot_general(both, onehot, NT, preferred_element_type=jnp.float32)
            out = out.astype(jnp.bfloat16)
            wide_hi[src, pl.ds(p * width, width), :] = out[:width]
            wide_lo[src, pl.ds(p * width, width), :] = out[width:]

    widen(r)

    @pl.when(c != 0)
    def _():
        raw_copy(0, c).wait_recv()
        for d in range(1, n_col):
            to = col_peer(d)

            @pl.when(to != 0)
            def _():
                raw_copy(to, c).start()

    def arrive(d, carry):
        src = lax.rem(r + n_row - d, n_row)
        label_copy(row_peer(1), src).wait_recv()
        for p in range(part_dev):
            piece_copy(row_peer(1), src, p).wait_recv()
        widen(src)
        return carry

    lax.fori_loop(1, n_row, arrive, 0)

    @pl.when(c != 0)
    def _():
        for half in range(2):
            q_forward(q_copy, half, 2, n_row - 1)

    def gather_owner(o):
        total = jnp.zeros((TILE, cols_dev), jnp.float32)
        for src in range(n_row):
            code = got_labels[src, pl.ds(part_dev, 1), :][:, : part_dev * width]
            spot = lax.broadcasted_iota(jnp.int32, (TILE, part_dev * width), 0) + o * TILE
            onehot = jnp.where(spot == code, 1.0, 0.0).astype(jnp.bfloat16)
            total += lax.dot_general(onehot, wide_hi[src], NN, preferred_element_type=jnp.float32)
            total += lax.dot_general(onehot, wide_lo[src], NN, preferred_element_type=jnp.float32)
        partial[o] = total

    def gather_pair(j, carry):
        gather_owner(2 * j + 1 - parity)
        pair_copy(j).start()
        return carry

    lax.fori_loop(0, pairs, gather_pair, 0)

    def gather_own(j, carry):
        owner = 2 * j + parity
        gather_owner(owner)
        pair_copy(j).wait_recv()
        partial[owner] = partial[owner] + paired[j]

        @pl.when(owner != c)
        def _():
            part_copy(j, place).start()

        return carry

    lax.fori_loop(0, pairs, gather_own, 0)

    own_tile.wait()
    tile_ref[...] = tile_ref[...] - partial[c]

    def collect(d, carry):
        slot = lax.rem(place + pairs - d, pairs)
        part_copy(lax.rem(place + 1, pairs), slot).wait_recv()
        tile_ref[...] = tile_ref[...] - landed[slot]
        return carry

    lax.fori_loop(1, pairs, collect, 0)

    @pl.when(c == 0)
    def _():
        top_ref[...] = tile_ref[:, :PANEL]
        for to in range(1, n_col):
            deal_copy(to).start()

    @pl.when(c != 0)
    def _():
        deal_copy(c).wait_recv()

    for half in range(2):

        @pl.when(r == half)
        def _():
            for d in range(1, n_row):
                lift_copy(row_peer(d), half).start()

    def top_sends(act):
        for d in range(1, n_col):
            to = col_peer(d)

            @pl.when(to != 0)
            def _():
                act(top_copy(to, c))

    top_sends(lambda copy: copy.start())

    for half in range(2):

        @pl.when(r != half)
        def _():
            lift_copy(row_peer(1), half).wait_recv()
            for d in range(1, n_col):
                diag_copy(col_peer(d), half, c).start()

    for half in range(2):

        @pl.when((r == half) & (c == 0))
        def _():
            q_ref[pl.ds(half * TILE, TILE), :] = tile_ref[...]
            q_out(q_rest_copy, half, lambda copy: copy.start())

    for half in range(2):

        @pl.when(c == 0)
        def _():
            q_forward(q_rest_copy, half, 0, n_row - 1)

    @pl.when(c != 0)
    def _():
        for d in range(1, n_col):
            index = col_peer(d)
            top_copy(index, index).wait_recv()

            @pl.when(index != 0)
            def _():
                raw_copy(index, index).wait_recv()

    for half in range(2):

        @pl.when(r == half)
        def _():
            diag_ref[pl.ds(half * TILE, TILE), :] = top_ref[...]

        @pl.when(r != half)
        def _():
            for d in range(1, n_col):
                index = col_peer(d)
                diag_copy(index, half, index).wait_recv()

        @pl.when(((r < half) | (r == n_row - 1)) & (c != 0))
        def _():
            q_copy(row_peer(1), half).wait_recv()

        @pl.when(((r < half) | (r == n_row - 1)) & (c == 0))
        def _():
            q_rest_copy(row_peer(1), half).wait_recv()

        @pl.when((r != half) & (c == 0))
        def _():
            q_ref[pl.ds(half * TILE, TILE), :PANEL] = diag_ref[pl.ds(half * TILE, TILE), :]

    for d in range(1, n_row):
        label_copy(row_peer(d), r).wait_send()
        for p in range(part_dev):
            piece_copy(row_peer(d), r, p).wait_send()

    @pl.when(c == 0)
    def _():
        for to in range(1, n_col):
            raw_deal(to).wait_send()
            deal_copy(to).wait_send()

    @pl.when(c != 0)
    def _():
        for d in range(1, n_col):
            to = col_peer(d)

            @pl.when(to != 0)
            def _():
                raw_copy(to, c).wait_send()

    for j in range(pairs):
        pair_copy(j).wait_send()

        @pl.when(j != place)
        def _():
            part_copy(j, place).wait_send()

    top_sends(lambda copy: copy.wait_send())
    for half in range(2):

        @pl.when(r == half)
        def _():
            for d in range(1, n_row):
                lift_copy(row_peer(d), half).wait_send()

        @pl.when(r != half)
        def _():
            for d in range(1, n_col):
                diag_copy(col_peer(d), half, c).wait_send()

        @pl.when((r == half) & (c != 0))
        def _():
            q_out(q_copy, half, lambda copy: copy.wait_send())

        @pl.when((r > half) & (r < n_row - 1) & (c != 0))
        def _():
            q_copy(r + 1, half).wait_send()

        @pl.when((r == half) & (c == 0))
        def _():
            q_out(q_rest_copy, half, lambda copy: copy.wait_send())

        @pl.when((r > half) & (r < n_row - 1) & (c == 0))
        def _():
            q_rest_copy(r + 1, half).wait_send()


def exchange(n_row, n_col, base, factors, coupling, positions, counts, owners):
    rows_dev, cols_dev = base.shape
    part_dev = coupling.shape[0]
    smem_spec = pl.BlockSpec(memory_space=pltpu.SMEM)
    any_spec = pl.BlockSpec(memory_space=pl.ANY)
    vmem_spec = pl.BlockSpec(memory_space=pltpu.VMEM)
    dma = pltpu.SemaphoreType.DMA
    return pl.pallas_call(
        functools.partial(exchange_kernel, n_row, n_col, part_dev),
        out_shape=(
            jax.ShapeDtypeStruct((rows_dev, PANEL), jnp.float32),
            jax.ShapeDtypeStruct((PANEL, cols_dev), jnp.float32),
            jax.ShapeDtypeStruct((PANEL, PANEL), jnp.float32),
            jax.ShapeDtypeStruct((TILE, PANEL), jnp.float32),
            jax.ShapeDtypeStruct((TILE, cols_dev), jnp.float32),
        ),
        in_specs=[any_spec, any_spec, any_spec, vmem_spec, smem_spec, smem_spec],
        out_specs=(any_spec, vmem_spec, vmem_spec, vmem_spec, vmem_spec),
        scratch_shapes=[
            pltpu.VMEM(factors.shape, factors.dtype),
            pltpu.VMEM(coupling.shape, coupling.dtype),
            pltpu.VMEM((n_row, KS * part_dev // n_row, KS), jnp.float32),
            pltpu.VMEM((n_row, 8, KS), jnp.int32),
            pltpu.VMEM((n_row, KS * part_dev // n_row, KS), jnp.float32),
            pltpu.VMEM((n_row, 8, KS), jnp.int32),
            pltpu.VMEM((n_row, KS * part_dev // n_row, cols_dev), jnp.bfloat16),
            pltpu.VMEM((n_row, KS * part_dev // n_row, cols_dev), jnp.bfloat16),
            pltpu.VMEM((n_col, TILE, cols_dev), jnp.float32),
            pltpu.VMEM((n_col // 2, TILE, cols_dev), jnp.float32),
            pltpu.VMEM((n_col // 2, TILE, cols_dev), jnp.float32),
            dma((n_row, part_dev)),
            dma((n_row, part_dev)),
            dma((n_row,)),
            dma((n_row,)),
            dma((n_col,)),
            dma((n_col,)),
            dma((2, n_row)),
            dma((2,)),
            dma((n_col // 2,)),
            dma((n_col // 2,)),
            dma((n_col // 2,)),
            dma((n_col // 2,)),
            dma((n_col,)),
            dma((n_col,)),
            dma((n_col,)),
            dma((n_row,)),
            dma((2,)),
            dma((2, n_col)),
            dma((2, n_col)),
            dma((5,)),
            dma((2, part_dev)),
        ],
        compiler_params=pltpu.CompilerParams(
            collective_id=0, has_side_effects=True, vmem_limit_bytes=VMEM_BYTES
        ),
    )(base, factors, coupling, positions, counts, owners)


def full_dot(a, b, dims):
    return lax.dot_general(
        a, b, dims, precision=lax.Precision.HIGHEST, preferred_element_type=jnp.float32
    )


def split_dot(a, b, dims):
    a_high = a.astype(jnp.bfloat16)
    a_low = (a - a_high.astype(jnp.float32)).astype(jnp.bfloat16)
    b_high = b.astype(jnp.bfloat16)
    b_low = (b - b_high.astype(jnp.float32)).astype(jnp.bfloat16)
    dot = functools.partial(
        lax.dot_general, dimension_numbers=dims, preferred_element_type=jnp.float32
    )
    return dot(a_high, b_high) + (dot(a_high, b_low) + dot(a_low, b_high))


STEP = 8


def cholesky_and_inverse(work, block):
    row = lax.broadcasted_iota(jnp.int32, (TILE, TILE), 0)
    col = lax.broadcasted_iota(jnp.int32, (TILE, TILE), 1)
    groups = TILE // 8
    left = block.reshape(groups, 8, TILE)
    right = jnp.where(row == col, 1.0, 0.0).reshape(groups, 8, TILE)
    for k in range(0, TILE, STEP):
        g = k // 8
        s = k % 8
        lanes_left = [
            jnp.broadcast_to(left[0:1, s + i : s + i + 1, :], (1, 8, TILE)) for i in range(STEP)
        ]
        lanes_right = [
            jnp.broadcast_to(right[0:1, s + i : s + i + 1, :], (1, 8, TILE)) for i in range(STEP)
        ]
        cols = [
            jnp.broadcast_to(left[:, :, k + i : k + i + 1], left.shape) for i in range(STEP)
        ]
        heads = [
            [
                jnp.broadcast_to(cols[j][0:1, s + i : s + i + 1, :], (1, 8, TILE))
                for j in range(i + 1)
            ]
            for i in range(STEP)
        ]
        for i in range(STEP):
            scale = lax.rsqrt(heads[i][i])
            lanes_left[i] = lanes_left[i] * scale
            lanes_right[i] = lanes_right[i] * scale
            cols[i] = cols[i] * scale
            below = {}
            for m in range(i + 1, STEP):
                below[m] = heads[m][i] * scale
            for m in range(i + 1, STEP):
                for j in range(i + 1, m + 1):
                    heads[m][j] = heads[m][j] - below[m] * below[j]
                lanes_left[m] = lanes_left[m] - below[m] * lanes_left[i]
                lanes_right[m] = lanes_right[m] - below[m] * lanes_right[i]
                cols[m] = cols[m] - cols[i] * below[m]
        for i in range(STEP):
            work[k + i : k + i + 1, :TILE] = lanes_left[i][0, 0:1, :]
            work[k + i : k + i + 1, TILE:] = lanes_right[i][0, 0:1, :]
        if s + STEP == 8:
            left, right = left[1:], right[1:]
            cols = [x[1:] for x in cols]
        if left.shape[0]:
            for i in range(STEP):
                left = left - cols[i] * lanes_left[i]
                right = right - cols[i] * lanes_right[i]
    upper = jnp.where(row <= col, work[:, :TILE], 0.0)
    inverse = jnp.where(row >= col, work[:, TILE:], 0.0)
    return upper.T, inverse


def factor_kernel(
    base_ref, raw_ref, q_ref, diag_ref, top_ref, tile_ref, out_ref, work, inverse, panel, q_full
):
    r = lax.axis_index("row")
    c = lax.axis_index("col")
    rows_dev, cols_dev = base_ref.shape
    lower0, inverse0 = cholesky_and_inverse(work, diag_ref[:TILE, :TILE])
    lower10 = full_dot(diag_ref[TILE:, :TILE], inverse0, NT)
    lower1, inverse1 = cholesky_and_inverse(
        work, diag_ref[TILE:, TILE:] - full_dot(lower10, lower10, NT)
    )
    inverse[:TILE, :TILE] = inverse0
    inverse[:TILE, TILE:] = jnp.zeros((TILE, TILE), jnp.float32)
    inverse[TILE:, TILE:] = inverse1
    inverse[TILE:, :TILE] = -full_dot(inverse1, full_dot(lower10, inverse0, NN), NN)
    q_full[...] = full_dot(inverse[...], q_ref[...], NN)
    raw_ref[:TILE, :] = top_ref[...]

    def rows(i, carry):
        at = pl.ds(pl.multiple_of(i * TILE, TILE), TILE)
        panel[at, :] = split_dot(raw_ref[at, :], inverse[...], NT)
        return carry

    lax.fori_loop(0, rows_dev // TILE, rows, 0)

    @pl.when(r == 0)
    def _():
        panel[:TILE, :TILE] = lower0
        panel[:TILE, TILE:] = jnp.zeros((TILE, TILE), jnp.float32)

    @pl.when(r == 1)
    def _():
        panel[:TILE, :TILE] = lower10
        panel[:TILE, TILE:] = lower1

    def trailing(i, carry):
        at = pl.ds(pl.multiple_of(i * TILE, TILE), TILE)
        current = jnp.where(i == c, tile_ref[...], base_ref[at, :])
        out_ref[at, :] = current - split_dot(panel[at, :], q_full[...], NN)
        return carry

    lax.fori_loop(0, rows_dev // TILE, trailing, 0)

    @pl.when(r < 2)
    def _():
        out_ref[:TILE, :] = jnp.zeros((TILE, cols_dev), jnp.float32)

    @pl.when(c == 0)
    def _():
        out_ref[:, :PANEL] = panel[...]


def factorise(base, raw, q, diag, top, tile):
    rows_dev, cols_dev = base.shape
    vmem_spec = pl.BlockSpec(memory_space=pltpu.VMEM)
    return pl.pallas_call(
        factor_kernel,
        out_shape=jax.ShapeDtypeStruct(base.shape, jnp.float32),
        in_specs=[vmem_spec] * 6,
        out_specs=vmem_spec,
        scratch_shapes=[
            pltpu.VMEM((TILE, 2 * TILE), jnp.float32),
            pltpu.VMEM((PANEL, PANEL), jnp.float32),
            pltpu.VMEM((rows_dev, PANEL), jnp.float32),
            pltpu.VMEM((PANEL, cols_dev), jnp.float32),
        ],
        compiler_params=pltpu.CompilerParams(vmem_limit_bytes=VMEM_BYTES),
    )(base, raw, q, diag, top, tile)


def local(base_matrix, inverse_factors, coupling, positions, counts, owners):
    n_row = lax.axis_size("row")
    n_col = lax.axis_size("col")
    raw, q, diag, top, tile = exchange(
        n_row, n_col, base_matrix, inverse_factors, coupling, positions, counts, owners
    )
    return factorise(base_matrix, raw, q, diag, top, tile)


def solution(mesh):
    in_specs = (
        P("row", "col"),
        P(("row", "col"), None, None, None),
        P(("row", "col"), None, None, None),
        P(("row", "col"), None),
        P(("row", "col"), None),
        P(("row", "col")),
    )
    out_specs = P("row", "col")
    return jax.shard_map(local, mesh=mesh, in_specs=in_specs, out_specs=out_specs, check_vma=False)
```
